256 devices in a mesh: chan: 32 (over x, y, core), tile: 8 (over z).
Axes of the slice: x: 4, y: 4, z: 8, core: 2. Of those that a mesh axis runs over, the one named last changes fastest.
Arguments:
- amp: bfloat16 [64, 2048, 768], P('chan', 'tile'), may hold values from -6 to 6
- v_pphh: bfloat16 [64, 2048, 768], P('chan', 'tile'), may hold values from -6 to 6
- v_pp: bfloat16 [64, 2048, 2048], P('chan', 'tile'), may hold values from -0.125 to 0.125
- w_ph: bfloat16 [64, 2048, 2048], P('chan', 'tile'), may hold values from -0.125 to 0.125
- coef: bfloat16 [64, 128], P('chan', 'tile'), may hold values from -1 to 1
- target: int32 [64, 128], P('chan', 'tile'), may hold values from 0 to 8191, as said below
- pp_size: int32 [64], P('chan'), may hold values from 16 to 2048
- e_part: float32 [64, 2048], P('chan', 'tile'), may hold values from 0.5 to 4
- e_hole: float32 [64, 768], P('chan'), may hold values from 0.5 to 4
Outputs:
- new_amp: bfloat16 [64, 2048, 768], P('chan', 'tile')
The draws below stay inside these ranges and needn't reach their ends.
Inputs may be any that keep to these rules, and one draw needn't show every extreme that they name: target is a one-to-one map of all row blocks onto all row blocks; block b goes to a block b2 with b2 // 16 == b // 16; for each value of b // 16, the channels of each group of 2 consecutive channels send exactly 2 * 16 // 32 blocks into each group of 2 consecutive channels.
All inputs are finite; a program needn't handle non-finite values.
Results may differ from the reference program's by a relative error of at most 0.002.
Values may be sent and summed in bfloat16 or wider, within the bound.
No kernel may reach another device: no remote copies, remote signals or barrier semaphores. Data moves between devices by JAX's collectives and lax.ppermute only.
A program may use at most 64 MiB of HBM per device.

```python
import math
import jax
import jax.numpy as jnp
from jax import lax

CH_DEV = 2
P_SIZE = 2048
H = 768
NB_T = 16
NB = 128
ROWS = 16
CH = 64
N_CHAN = 32
N_TILE = 8


def draw_target(key, part):
    key = jax.random.fold_in(key, 7)
    items = CH_DEV * NB_T
    per_peer = items // N_CHAN
    key_first, key_second = jax.random.split(key)
    keys_first = jax.random.split(key_first, N_TILE * N_CHAN)
    keys_second = jax.random.split(key_second, N_TILE * N_CHAN)
    first = jax.vmap(lambda k: jax.random.permutation(k, items))(keys_first).reshape(N_TILE, N_CHAN, items)
    second = jax.vmap(lambda k: jax.random.permutation(k, items))(keys_second).reshape(N_TILE, N_CHAN, items)
    dest = first // per_peer
    incoming = jnp.arange(N_CHAN)[None, :, None] * per_peer + first % per_peer
    tiles = jnp.arange(N_TILE)[:, None, None]
    slot = second[tiles, dest, incoming]
    channel = dest * CH_DEV + slot // NB_T
    block = tiles * NB_T + slot % NB_T
    value = channel * NB + block
    value = value.reshape(N_TILE, N_CHAN, CH_DEV, NB_T).transpose(1, 2, 0, 3).reshape(CH, NB)
    return value.astype(jnp.int32)


def set_ends(values, stream_key, smallest, largest):
    longest = values.shape.index(max(values.shape))
    spots = []
    for shift in (0, 1):
        where = [jax.random.randint(jax.random.fold_in(stream_key, axis), (), 0, length) for axis, length in enumerate(values.shape)]
        where[longest] = (where[longest] + shift) % values.shape[longest]
        spots.append(tuple(where))
    return values.at[spots[0]].set(smallest).at[spots[1]].set(largest)


def block_levels(own_key, dims, pieces, smallest, largest):
    level, own = 1.0, jax.random.fold_in(own_key, 6)
    for dim, shards_of in pieces:
        heights = jnp.exp(jax.random.uniform(jax.random.fold_in(own, dim), (shards_of,), jnp.float32, smallest / len(pieces), largest / len(pieces)))
        level = level * jnp.repeat(heights, dims[dim] // shards_of).reshape([-1 if axis == dim else 1 for axis in range(len(dims))])
    return level


def normal_values(rng, shape, scale, reach, cuts=(), kind=jnp.bfloat16):
    result = jax.random.normal(rng, shape, jnp.float32) * scale
    if len(cuts) > 0:
        result = block_levels(rng, shape, cuts, -0.22, 0.18) * result
    return jnp.clip(result, min=-reach, max=reach).astype(kind)


def setup_inputs(seed: int = 0) -> dict:
    splits = jax.random.split(jax.random.key(seed), 10)
    return {
        "amp": normal_values(splits[0], (CH, P_SIZE, H), 1.0, 6.0, ((0, 32), (1, 8))),
        "v_pphh": normal_values(splits[1], (CH, P_SIZE, H), 1.0, 6.0, ((0, 32), (1, 8))),
        "v_pp": normal_values(splits[2], (CH, P_SIZE, P_SIZE), P_SIZE ** -0.5, 0.125, ((0, 32), (1, 8))),
        "w_ph": normal_values(splits[3], (CH, P_SIZE, P_SIZE), P_SIZE ** -0.5, 0.125, ((0, 32), (1, 8))),
        "coef": jnp.clip(jax.random.uniform(splits[4], (CH, NB), jnp.float32, -1.0, 1.0) * block_levels(splits[4], (CH, NB), ((0, 32), (1, 8)), -0.4, 0.0), -1.0, 1.0).astype(jnp.bfloat16),
        "target": draw_target(jax.random.fold_in(splits[9], 71), 0),
        "pp_size": set_ends(jax.random.randint(splits[6], (CH,), ROWS, P_SIZE + 1), jax.random.fold_in(splits[6], 1), ROWS, P_SIZE).astype(jnp.int32),
        "e_part": jnp.clip(jnp.exp(math.log(4.0) - 2.0794415 * jax.random.uniform(splits[7], (CH, P_SIZE), jnp.float32) ** block_levels(splits[7], (CH, P_SIZE), ((0, 32), (1, 8)), -0.2, 0.2)), 0.5, 4.0),
        "e_hole": jnp.clip(jnp.exp(math.log(4.0) - 2.0794415 * jax.random.uniform(splits[8], (CH, H), jnp.float32) ** block_levels(splits[8], (CH, H), ((0, 32),), -0.2, 0.2)), 0.5, 4.0),
    }


def channel_products(left, right):
    def one(pair):
        return jnp.dot(pair[0].astype(jnp.float32), pair[1].astype(jnp.float32))
    return lax.map(one, (left, right))


def reference(amp, v_pphh, v_pp, w_ph, coef, target, pp_size, e_part, e_hole):
    count, rows_all, width = amp.shape
    blocks = target.shape[1]
    rows = rows_all // blocks
    ladder = channel_products(v_pp, amp)
    flat_coef = coef.reshape(-1).astype(jnp.float32)
    flat_target = target.reshape(-1).astype(jnp.int32)
    items = (amp.reshape(count * blocks, rows, width).astype(jnp.float32) * flat_coef[:, None, None]).astype(jnp.bfloat16)
    recoupled = jnp.zeros_like(items).at[flat_target].set(items).reshape(count, rows_all, width)
    cycle = channel_products(w_ph, recoupled).astype(jnp.bfloat16)
    back = cycle.reshape(count * blocks, rows, width)[flat_target].astype(jnp.float32)
    cycle_term = (flat_coef[:, None, None] * back).reshape(count, rows_all, width)
    total = v_pphh.astype(jnp.float32) + ladder + cycle_term
    denom = e_part[:, :, None] + e_hole[:, None, :]
    live = jnp.arange(rows_all, dtype=jnp.int32)[None, :] < pp_size[:, None]
    return jnp.where(live[:, :, None], total / denom, jnp.float32(0.0)).astype(jnp.bfloat16)
```

```python
import functools

import jax
import jax.numpy as jnp
from jax import lax
from jax.experimental import pallas as pl
from jax.experimental.pallas import tpu as pltpu
from jax.sharding import PartitionSpec as P

META = 128
NEAR = 512
VMEM_LIMIT = 56 * 1024 * 1024

F32, BF16, I32 = jnp.float32, jnp.bfloat16, jnp.int32


def call(kernel, outs, operands, scalars, scratch=(), flops=0, moved=0):
    smem, vmem = pl.BlockSpec(memory_space=pltpu.SMEM), pl.BlockSpec(memory_space=pltpu.VMEM)
    return pl.pallas_call(
        kernel,
        out_shape=outs,
        in_specs=[smem] * len(scalars) + [vmem] * len(operands),
        out_specs=jax.tree.map(lambda _: vmem, outs),
        scratch_shapes=list(scratch),
        compiler_params=pltpu.CompilerParams(vmem_limit_bytes=VMEM_LIMIT),
        cost_estimate=pl.CostEstimate(flops=flops, bytes_accessed=moved, transcendentals=0),
    )(*scalars, *operands)


def pack_kernel(blocks, ch_dev, own, slot, coef, where, amp, items, near):
    count, rows, width = amp.shape
    near_width = near.shape[2]
    lane = lax.broadcasted_iota(I32, (rows, META), 1)
    place = lax.broadcasted_iota(I32, (rows, 2 * META), 0)
    place += rows * (lax.broadcasted_iota(I32, (rows, 2 * META), 1) // META)
    names = jnp.zeros((rows, 2 * META), F32)
    for b in range(count):
        to = own[b]
        block = amp[b]
        items[to, :, :width] = (block.astype(F32) * coef[b]).astype(BF16)
        note = jnp.where(lane < META // 2, slot[b].astype(F32), coef[b])
        items[to, :, width:] = note.astype(BF16)
        near[to] = block[:, :near_width]
        names = jnp.where(place == to, where[b].astype(F32), names)
    near[count] = jnp.zeros((rows, near_width), BF16)
    near[count, :, : 2 * META] = names.astype(BF16)


def settle_kernel(slot, got, far):
    count, rows, wide = got.shape
    width = wide - META
    far_width = far.shape[2]
    row = lax.broadcasted_iota(I32, (rows, META), 0)
    notes = [jnp.zeros((rows, META), BF16)] * 2
    for c in range(count):
        far[slot[c]] = got[c, :, width - far_width : width]
        note = got[c, :, width:].astype(F32)
        kept = notes[c // rows].astype(F32)
        notes[c // rows] = jnp.where(row == c % rows, note, kept).astype(BF16)
    for part in range(2):
        far[count, :, part * META : (part + 1) * META] = notes[part]


def cycle_kernel(tiles, row, coef, home, own, pair_a, pair_b, pair_c, last, *rest):
    far, (w_ph, back, placed, result) = rest[:-4], rest[-4:]
    count, rows, width = back.shape
    near = last.shape[2]
    ch_dev, total, _ = placed.shape
    per = total // len(far)

    def put(piece, c, block):
        at = row[piece * count + c]
        scaled = (block.astype(F32) * coef[piece * count + c]).astype(BF16)
        placed[at // total, pl.ds(pl.multiple_of(at % total, rows), rows), :near] = scaled

    def step(c, carry):
        at = row[c]
        placed[at // total, pl.ds(pl.multiple_of(at % total, rows), rows), :near] = own[c, :, :near]
        for i, pair in enumerate((pair_a, pair_b, pair_c)):
            put(2 * i + 1, c, pair[c, 0])
            put(2 * i + 2, c, pair[c, 1])
        put(7, c, last[c])
        return carry

    lax.fori_loop(0, count, step, 0, unroll=2)
    each = count // ch_dev
    for piece, ref in enumerate(far):
        at = pl.ds(pl.multiple_of(tiles[piece] * per, per), per)
        for ch in range(ch_dev):
            block = ref[ch * each : (ch + 1) * each]
            placed[ch, at, near:] = block.reshape(per, width - near)
    for ch in range(ch_dev):
        result[ch] = jnp.dot(w_ph[ch], placed[ch], preferred_element_type=F32).astype(BF16)
    for c in range(count):
        at = home[c]
        back[c] = result[at // each, pl.ds(pl.multiple_of(at % each * rows, rows), rows), :]


def near_kernel(row, *refs):
    pieces, (v_pp, ladder, placed) = refs[:-3], refs[-3:]
    ch_dev, total, _ = placed.shape
    count, rows = pieces[0].shape[0] - 1, pieces[0].shape[1]

    def step(c, carry):
        for piece, ref in enumerate(pieces):
            at = row[piece * count + c]
            placed[at // total, pl.ds(pl.multiple_of(at % total, rows), rows), :] = ref[c]
        return carry

    lax.fori_loop(0, count, step, 0, unroll=2)
    for ch in range(ch_dev):
        ladder[ch] = jnp.dot(v_pp[ch], placed[ch], preferred_element_type=F32)


def final_kernel(own, live, coef, far, v_pp, ladder, back, v_pphh, e_part, e_hole, out):
    ch_dev, per, width = out.shape
    count, rows, _ = back.shape
    near = ladder.shape[2]
    each = count // ch_dev
    for ch in range(ch_dev):
        more = jnp.dot(v_pp[ch], far[ch], preferred_element_type=F32)
        for b in range(each):
            i = ch * each + b
            at = slice(b * rows, (b + 1) * rows)
            come = back[own[i]].astype(F32) * coef[i]
            sums = jnp.concatenate([ladder[ch, at], more[at]], axis=1)
            sums = v_pphh[ch, at].astype(F32) + sums + come
            denom = e_part[ch, at] + e_hole[ch]
            row = lax.broadcasted_iota(I32, (rows, width), 0) + b * rows
            out[ch, at] = jnp.where(row < live[ch], sums / denom, 0.0).astype(BF16)


def body(amp, v_pphh, v_pp, w_ph, coef, target, pp_size, e_part, e_hole):
    ch_dev, tile_rows, width = amp.shape
    nb_tile = target.shape[1]
    rows = tile_rows // nb_tile
    n_tile = lax.axis_size("tile")
    blocks = nb_tile * n_tile
    count = ch_dev * nb_tile
    far_width = width - NEAR
    total = tile_rows * n_tile
    me = lax.axis_index("tile")
    right = [(i, (i + 1) % n_tile) for i in range(n_tile)]
    left = [((i + 1) % n_tile, i) for i in range(n_tile)]
    to_right = functools.partial(lax.ppermute, axis_name="tile", perm=right)
    to_left = functools.partial(lax.ppermute, axis_name="tile", perm=left)
    exchange = functools.partial(
        lax.all_to_all, axis_name="chan", split_axis=0, concat_axis=0, tiled=True
    )

    flat_target = target.reshape(-1)
    flat_coef = coef.reshape(-1).astype(F32)
    own = flat_target // (ch_dev * blocks)
    slot = flat_target % (ch_dev * blocks)
    index = jnp.arange(count, dtype=I32)
    where = index // nb_tile * blocks + me * nb_tile + index % nb_tile

    def row_of(names):
        return names // blocks * total + names % blocks * rows

    items, near = call(
        functools.partial(pack_kernel, blocks, ch_dev),
        (
            jax.ShapeDtypeStruct((count, rows, width + META), BF16),
            jax.ShapeDtypeStruct((count + 1, rows, NEAR), BF16),
        ),
        (amp.reshape(count, rows, width),),
        (own, slot, flat_coef, where),
    )
    r1, l1 = to_right(near), to_left(near)
    got = exchange(items)
    got_slot = got[:, 0, width].astype(I32)
    home = got_slot // blocks * nb_tile + got_slot % nb_tile
    far = call(
        settle_kernel,
        jax.ShapeDtypeStruct((count + 1, rows, far_width), BF16),
        (got,),
        (home,),
    )
    fr1, fl1 = to_right(far), to_left(far)
    r2, l2 = to_right(r1), to_left(l1)
    fr2, fl2 = to_right(fr1), to_left(fl1)
    r3, l3 = to_right(r2), to_left(l2)
    fr3, fl3 = to_right(fr2), to_left(fl2)
    r4 = to_right(r3)
    fl4 = to_left(fl3)

    def pair(a, b):
        return exchange(jnp.stack([a[:count], b[:count]], axis=1))

    got_a, got_b, got_c = pair(r1, l1), pair(r2, l2), pair(r3, l3)
    got_d = exchange(r4[:count])

    near_all = (near, r1, l1, r2, l2, r3, l3, r4)
    far_all = (far, fr1, fl1, fr2, fl2, fr3, fl3, fl4)
    steps = jnp.array([0, -1, 1, -2, 2, -3, 3, 4], dtype=I32)
    tiles = (me + steps + n_tile) % n_tile

    def notes(pieces, lane):
        kept = jnp.stack([p[count, :, : 2 * META] for p in pieces])
        kept = kept.reshape(len(pieces), rows, 2, META)[:, :, :, lane]
        return kept.transpose(0, 2, 1).reshape(-1)

    back = call(
        cycle_kernel,
        jax.ShapeDtypeStruct((count, rows, width), BF16),
        (got, got_a, got_b, got_c, got_d, *far_all, w_ph),
        (
            tiles,
            row_of(notes(far_all, 0).astype(I32)),
            notes(far_all, META // 2).astype(F32),
            home,
        ),
        scratch=(
            pltpu.VMEM((ch_dev, total, width), BF16),
            pltpu.VMEM((ch_dev, tile_rows, width), BF16),
        ),
        flops=2 * ch_dev * tile_rows * total * width,
        moved=20 * 2**20,
    )
    returned = exchange(back)

    ladder = call(
        near_kernel,
        jax.ShapeDtypeStruct((ch_dev, tile_rows, NEAR), F32),
        (*near_all, v_pp),
        (row_of(notes(near_all, 0).astype(I32)),),
        scratch=(pltpu.VMEM((ch_dev, total, NEAR), BF16),),
        flops=2 * ch_dev * tile_rows * total * NEAR,
        moved=10 * 2**20,
    )
    whole_far = lax.all_gather(amp[:, :, NEAR:], "tile", axis=1, tiled=True)
    return call(
        final_kernel,
        jax.ShapeDtypeStruct((ch_dev, tile_rows, width), BF16),
        (
            whole_far,
            v_pp,
            ladder,
            returned,
            v_pphh,
            e_part[:, :, None],
            e_hole[:, None, :],
        ),
        (own, pp_size - me * tile_rows, flat_coef),
        flops=2 * ch_dev * tile_rows * total * far_width,
        moved=10 * 2**20,
    )


def solution(mesh):
    placed = (
        P("chan", "tile", None),
        P("chan", "tile", None),
        P("chan", "tile", None),
        P("chan", "tile", None),
        P("chan", "tile"),
        P("chan", "tile"),
        P("chan"),
        P("chan", "tile"),
        P("chan", None),
    )
    return jax.shard_map(
        body, mesh=mesh, in_specs=placed, out_specs=P("chan", "tile", None), check_vma=False
    )
```

```python
import functools

import jax
import jax.numpy as jnp
from jax import lax
from jax.experimental import pallas as pl
from jax.experimental.pallas import tpu as pltpu
from jax.sharding import PartitionSpec as P

META = 128
VMEM_LIMIT = 56 * 1024 * 1024

F32, BF16, I32 = jnp.float32, jnp.bfloat16, jnp.int32


def call(kernel, outs, operands, scalars=(), scratch=(), flops=0, moved=0):
    smem, vmem = pl.BlockSpec(memory_space=pltpu.SMEM), pl.BlockSpec(memory_space=pltpu.VMEM)
    return pl.pallas_call(
        kernel,
        out_shape=outs,
        in_specs=[smem] * len(scalars) + [vmem] * len(operands),
        out_specs=jax.tree.map(lambda _: vmem, outs),
        scratch_shapes=list(scratch),
        compiler_params=pltpu.CompilerParams(vmem_limit_bytes=VMEM_LIMIT),
        cost_estimate=pl.CostEstimate(flops=flops, bytes_accessed=moved, transcendentals=0),
    )(*scalars, *operands)


def tables(count):
    return (
        pltpu.VMEM((count, 8, META), I32),
        pltpu.SMEM((count, 8, META), I32),
        pltpu.SemaphoreType.DMA,
    )


def to_scalars(vector, scalar, sem):
    copy = pltpu.make_async_copy(vector, scalar, sem)
    copy.start()
    copy.wait()


def pack_kernel(blocks, target, coef, amp, items):
    count, rows, width = amp.shape
    ch_dev, nb_tile = target.shape
    factor = coef[...].astype(F32)
    for b in range(count):
        ch, j = divmod(b, nb_tile)
        to = lax.div(target[ch, j], ch_dev * blocks)
        slot = lax.rem(target[ch, j], ch_dev * blocks)
        scaled = amp[b].astype(F32) * factor[ch : ch + 1, j : j + 1]
        items[to, :, :width] = scaled.astype(BF16)
        items[to, :, width:] = jnp.full((rows, META), slot.astype(F32)).astype(BF16)


def settle_kernel(blocks, got, placed, homes, slot_v, slot, sem):
    count, rows, wide = got.shape
    width = wide - META
    nb_tile = count // 2
    lane = lax.broadcasted_iota(I32, (rows, META), 1)
    notes = jnp.zeros((rows, META), F32)
    for c in range(count):
        notes = jnp.where(lane == c, got[c, :, width:].astype(F32), notes)
    at = notes[:8].astype(I32)
    homes[...] = lax.div(at, blocks) * nb_tile + lax.rem(at, nb_tile)
    slot_v[0] = homes[...]
    to_scalars(slot_v, slot, sem)
    for c in range(count):
        placed[slot[0, 0, c]] = got[c, :, :width]


def tile_at(step):
    n = lax.axis_size("tile")
    return lax.rem(lax.axis_index("tile") + step + n, n)


STEPS = (0, -1, 1, -2, 2, -3, 3, 4)


def gather_rows(pieces, placed):
    ch_dev, total, width = placed.shape
    per = total // len(STEPS)
    each = pieces[0].shape[0] // ch_dev
    for piece, ref in enumerate(pieces):
        at = pl.ds(pl.multiple_of(tile_at(STEPS[piece]) * per, per), per)
        for ch in range(ch_dev):
            placed[ch, at] = ref[ch * each : (ch + 1) * each].reshape(per, width)
    at = pl.ds(pl.multiple_of(tile_at(STEPS[-1]) * per, per), per)
    for ch in range(ch_dev):
        placed[ch, at] = jnp.zeros((per, width), BF16)


def most_kernel(*refs):
    pieces, (matrix, part, placed) = refs[: len(STEPS) - 1], refs[len(STEPS) - 1 :]
    gather_rows(pieces, placed)
    for ch in range(placed.shape[0]):
        part[ch] = jnp.dot(matrix[ch], placed[ch], preferred_element_type=F32)


def rest_of(ch, halves, matrix):
    per, width = matrix.shape[1], halves[0].shape[2]
    columns = pl.ds(pl.multiple_of(tile_at(STEPS[-1]) * per, per), per)
    last = halves[ch][...].reshape(per, width)
    return jnp.dot(matrix[ch, :, columns], last, preferred_element_type=F32)


def back_kernel(homes, half_a, half_b, part, w_ph, back, result, slot_v, slot, sem):
    count, rows, _ = back.shape
    ch_dev, per, width = part.shape
    slot_v[0] = homes[...]
    to_scalars(slot_v, slot, sem)
    for ch in range(ch_dev):
        total = part[ch] + rest_of(ch, (half_a, half_b), w_ph)
        result[ch * per : (ch + 1) * per] = total.astype(BF16)
    for c in range(count):
        row = pl.ds(pl.multiple_of(slot[0, 0, c] * rows, rows), rows)
        back[c] = result[row, :]


def ladder_kernel(half_a, half_b, part, v_pp, v_pphh, ladder):
    for ch in range(part.shape[0]):
        total = part[ch] + rest_of(ch, (half_a, half_b), v_pp)
        ladder[ch] = v_pphh[ch].astype(F32) + total


def final_kernel(blocks, target, live, coef, ladder, back, e_part, e_hole, out):
    ch_dev, per, width = out.shape
    count, rows, _ = back.shape
    nb_tile = count // ch_dev
    first = lax.axis_index("tile") * per
    factor = coef[...].astype(F32)
    for ch in range(ch_dev):
        for b in range(nb_tile):
            at = slice(b * rows, (b + 1) * rows)
            own = lax.div(target[ch, b], ch_dev * blocks)
            come = back[own].astype(F32) * factor[ch : ch + 1, b : b + 1]
            sums = ladder[ch, at] + come
            denom = e_part[ch, at] + e_hole[ch]
            row = lax.broadcasted_iota(I32, (rows, width), 0) + (first + b * rows)
            out[ch, at] = jnp.where(row < live[ch], sums / denom, 0.0).astype(BF16)


def after(x, *others):
    return lax.optimization_barrier((x, *others))[0]


def body(amp, v_pphh, v_pp, w_ph, coef, target, pp_size, e_part, e_hole):
    ch_dev, tile_rows, width = amp.shape
    nb_tile = target.shape[1]
    rows = tile_rows // nb_tile
    n_tile = lax.axis_size("tile")
    blocks = nb_tile * n_tile
    count = ch_dev * nb_tile
    total = tile_rows * n_tile
    right = [(i, (i + 1) % n_tile) for i in range(n_tile)]
    left = [((i + 1) % n_tile, i) for i in range(n_tile)]
    to_right = functools.partial(lax.ppermute, axis_name="tile", perm=right)
    to_left = functools.partial(lax.ppermute, axis_name="tile", perm=left)

    def both(a, b):
        return to_right(a), to_left(b)

    exchange = functools.partial(
        lax.all_to_all, axis_name="chan", split_axis=0, concat_axis=0, tiled=True
    )

    own_rows = amp.reshape(count, rows, width)
    block_type = jax.ShapeDtypeStruct((count, rows, width), BF16)
    part_type = jax.ShapeDtypeStruct((ch_dev, tile_rows, width), F32)
    amp1 = both(own_rows, own_rows)
    items = call(
        functools.partial(pack_kernel, blocks),
        jax.ShapeDtypeStruct((count, rows, width + META), BF16),
        (coef, own_rows),
        (target,),
        moved=4 * 2**20,
    )
    far, homes = call(
        functools.partial(settle_kernel, blocks),
        (block_type, jax.ShapeDtypeStruct((8, META), I32)),
        (after(exchange(items), amp1),),
        scratch=tables(1),
        moved=4 * 2**20,
    )
    far1 = both(far, far)
    amp2 = both(*after(amp1))
    far2 = both(*after(far1))
    far3 = both(*after(far2))
    far4 = both(far3[0][: count // 2], far3[1][count // 2 :])
    def most(pieces, matrix):
        return call(
            most_kernel,
            part_type,
            (*pieces, matrix),
            scratch=(pltpu.VMEM((ch_dev, total, width), BF16),),
            flops=2 * ch_dev * tile_rows * total * width,
            moved=12 * 2**20,
        )

    cycle_most = most((far, *far1, *far2, *far3), w_ph)
    amp3 = both(*after(amp2, cycle_most, far4))
    back = call(
        back_kernel,
        block_type,
        (homes, *far4, cycle_most, w_ph),
        scratch=(pltpu.VMEM((ch_dev * tile_rows, width), BF16), *tables(1)),
        flops=2 * ch_dev * tile_rows * tile_rows * width,
        moved=6 * 2**20,
    )
    returned = exchange(back)
    amp3 = after(amp3, back)
    amp4 = both(amp3[0][: count // 2], amp3[1][count // 2 :])
    ladder = call(
        ladder_kernel,
        part_type,
        (*amp4, most((own_rows, *amp1, *amp2, *amp3), v_pp), v_pp, v_pphh),
        flops=2 * ch_dev * tile_rows * tile_rows * width,
        moved=6 * 2**20,
    )
    return call(
        functools.partial(final_kernel, blocks),
        jax.ShapeDtypeStruct((ch_dev, tile_rows, width), BF16),
        (coef, ladder, returned, e_part[:, :, None], e_hole[:, None, :]),
        (target, pp_size),
        flops=10 * ch_dev * tile_rows * width,
        moved=6 * 2**20,
    )


def solution(mesh):
    placed = (
        P("chan", "tile", None),
        P("chan", "tile", None),
        P("chan", "tile", None),
        P("chan", "tile", None),
        P("chan", "tile"),
        P("chan", "tile"),
        P("chan"),
        P("chan", "tile"),
        P("chan", None),
    )
    return jax.shard_map(
        body, mesh=mesh, in_specs=placed, out_specs=P("chan", "tile", None), check_vma=False
    )
```

```python
import functools

import jax
import jax.numpy as jnp
from jax import lax
from jax.experimental import pallas as pl
from jax.experimental.pallas import tpu as pltpu
from jax.sharding import PartitionSpec as P

META = 128
VMEM_LIMIT = 56 * 1024 * 1024

F32, BF16, I32 = jnp.float32, jnp.bfloat16, jnp.int32


def call(kernel, outs, operands, scalars=(), scratch=(), flops=0, moved=0):
    smem, vmem = pl.BlockSpec(memory_space=pltpu.SMEM), pl.BlockSpec(memory_space=pltpu.VMEM)
    return pl.pallas_call(
        kernel,
        out_shape=outs,
        in_specs=[smem] * len(scalars) + [vmem] * len(operands),
        out_specs=jax.tree.map(lambda _: vmem, outs),
        scratch_shapes=list(scratch),
        compiler_params=pltpu.CompilerParams(vmem_limit_bytes=VMEM_LIMIT),
        cost_estimate=pl.CostEstimate(flops=flops, bytes_accessed=moved, transcendentals=0),
    )(*scalars, *operands)


def tables(count):
    return (
        pltpu.VMEM((count, 8, META), I32),
        pltpu.SMEM((count, 8, META), I32),
        pltpu.SemaphoreType.DMA,
    )


def to_scalars(vector, scalar, sem):
    copy = pltpu.make_async_copy(vector, scalar, sem)
    copy.start()
    copy.wait()


def pack_kernel(blocks, target, coef, amp, items):
    count, rows, width = amp.shape
    ch_dev, nb_tile = target.shape
    factor = coef[...].astype(F32)
    for b in range(count):
        ch, j = divmod(b, nb_tile)
        to = lax.div(target[ch, j], ch_dev * blocks)
        slot = lax.rem(target[ch, j], ch_dev * blocks)
        scaled = amp[b].astype(F32) * factor[ch : ch + 1, j : j + 1]
        items[to, :, :width] = scaled.astype(BF16)
        items[to, :, width:] = jnp.full((rows, META), slot.astype(F32)).astype(BF16)


def settle_kernel(blocks, got, part_a, part_b, homes, placed, slot_v, slot, sem):
    count, rows, wide = got.shape
    width = wide - META
    nb_tile = count // 2
    lane = lax.broadcasted_iota(I32, (rows, META), 1)
    notes = jnp.zeros((rows, META), F32)
    for c in range(count):
        notes = jnp.where(lane == c, got[c, :, width:].astype(F32), notes)
    at = notes[:8].astype(I32)
    homes[...] = lax.div(at, blocks) * nb_tile + lax.rem(at, nb_tile)
    slot_v[0] = homes[...]
    to_scalars(slot_v, slot, sem)
    for c in range(count):
        placed[slot[0, 0, c]] = got[c, :, :width]
    part_a[...] = placed[: count // 2]
    part_b[...] = placed[count // 2 :]


def tile_at(step):
    n = lax.axis_size("tile")
    return lax.rem(lax.axis_index("tile") + step + n, n)


STEPS = (0, -1, 1, -2, 2, -3, 3, 4)


def most_kernel(*refs):
    pieces, (matrix, part, placed) = refs[:-3], refs[-3:]
    ch_dev, total, width = placed.shape
    near = len(STEPS) - 1
    per = total // len(STEPS)
    split = len(pieces) == ch_dev * near
    each = per // pieces[0].shape[1]
    for ch in range(ch_dev):
        for i, step in enumerate(STEPS[:-1]):
            at = pl.ds(pl.multiple_of(tile_at(step) * per, per), per)
            ref = pieces[ch * near + i] if split else pieces[i]
            block = ref[...] if split else ref[ch * each : (ch + 1) * each]
            placed[ch, at] = block.reshape(per, width)
        at = pl.ds(pl.multiple_of(tile_at(STEPS[-1]) * per, per), per)
        placed[ch, at] = jnp.zeros((per, width), BF16)
    for ch in range(ch_dev):
        part[ch] = jnp.dot(matrix[ch], placed[ch], preferred_element_type=F32)


def rest_of(ch, halves, matrix):
    per, width = matrix.shape[1], halves[0].shape[2]
    columns = pl.ds(pl.multiple_of(tile_at(STEPS[-1]) * per, per), per)
    last = halves[ch][...].reshape(per, width)
    return jnp.dot(matrix[ch, :, columns], last, preferred_element_type=F32)


def back_kernel(homes, half_a, half_b, part, w_ph, back, result, slot_v, slot, sem):
    count, rows, _ = back.shape
    ch_dev, per, width = part.shape
    slot_v[0] = homes[...]
    to_scalars(slot_v, slot, sem)
    for ch in range(ch_dev):
        total = part[ch] + rest_of(ch, (half_a, half_b), w_ph)
        result[ch * per : (ch + 1) * per] = total.astype(BF16)
    for c in range(count):
        row = pl.ds(pl.multiple_of(slot[0, 0, c] * rows, rows), rows)
        back[c] = result[row, :]


def final_kernel(
    blocks, target, live, coef, half_a, half_b, part, v_pp, back, v_pphh, e_part, e_hole, out
):
    ch_dev, per, width = out.shape
    count, rows, _ = back.shape
    nb_tile = count // ch_dev
    first = lax.axis_index("tile") * per
    factor = coef[...].astype(F32)
    for ch in range(ch_dev):
        more = rest_of(ch, (half_a, half_b), v_pp)
        for b in range(nb_tile):
            at = slice(b * rows, (b + 1) * rows)
            own = lax.div(target[ch, b], ch_dev * blocks)
            come = back[own].astype(F32) * factor[ch : ch + 1, b : b + 1]
            sums = v_pphh[ch, at].astype(F32) + (part[ch, at] + more[at]) + come
            denom = e_part[ch, at] + e_hole[ch]
            row = lax.broadcasted_iota(I32, (rows, width), 0) + (first + b * rows)
            out[ch, at] = jnp.where(row < live[ch], sums / denom, 0.0).astype(BF16)


def after(x, *others):
    return lax.optimization_barrier((x, *others))[0]


def body(amp, v_pphh, v_pp, w_ph, coef, target, pp_size, e_part, e_hole):
    ch_dev, tile_rows, width = amp.shape
    nb_tile = target.shape[1]
    rows = tile_rows // nb_tile
    n_tile = lax.axis_size("tile")
    blocks = nb_tile * n_tile
    count = ch_dev * nb_tile
    total = tile_rows * n_tile
    right = [(i, (i + 1) % n_tile) for i in range(n_tile)]
    left = [((i + 1) % n_tile, i) for i in range(n_tile)]
    to_right = functools.partial(lax.ppermute, axis_name="tile", perm=right)
    to_left = functools.partial(lax.ppermute, axis_name="tile", perm=left)

    def both(a, b):
        return to_right(a), to_left(b)

    exchange = functools.partial(
        lax.all_to_all, axis_name="chan", split_axis=0, concat_axis=0, tiled=True
    )

    own_rows = amp.reshape(count, rows, width)
    block_type = jax.ShapeDtypeStruct((count, rows, width), BF16)
    part_type = jax.ShapeDtypeStruct((ch_dev, tile_rows, width), F32)
    half = count // ch_dev
    amp_a, amp_b = own_rows[:half], own_rows[half:]
    a1, b1 = both(amp_a, amp_a), both(amp_b, amp_b)
    amp1 = tuple(jnp.concatenate(x, axis=0) for x in zip(a1, b1))
    items = call(
        functools.partial(pack_kernel, blocks),
        jax.ShapeDtypeStruct((count, rows, width + META), BF16),
        (coef, own_rows),
        (target,),
        moved=4 * 2**20,
    )
    half_type = jax.ShapeDtypeStruct((count // ch_dev, rows, width), BF16)
    far_a, far_b, homes = call(
        functools.partial(settle_kernel, blocks),
        (half_type, half_type, jax.ShapeDtypeStruct((8, META), I32)),
        (after(exchange(items), a1),),
        scratch=(pltpu.VMEM((count, rows, width), BF16), *tables(1)),
        flops=10**14,
        moved=4 * 2**20,
    )
    fa1, fb1 = both(*after((far_a, far_a), b1)), both(far_b, far_b)
    amp2 = both(*after(amp1))
    fa2, fb2 = both(*fa1), both(*fb1)
    fa3, fb3 = both(*fa2), both(*fb2)
    far4 = to_right(fa3[0]), to_left(fb3[1])

    def most(pieces, matrix):
        return call(
            most_kernel,
            part_type,
            (*pieces, matrix),
            scratch=(pltpu.VMEM((ch_dev, total, width), BF16),),
            flops=2 * ch_dev * tile_rows * total * width,
            moved=12 * 2**20,
        )

    cycle_most = most((far_a, *fa1, *fa2, *fa3, far_b, *fb1, *fb2, *fb3), w_ph)
    amp3 = both(*after(amp2, cycle_most, far4))
    back = call(
        back_kernel,
        block_type,
        (homes, *far4, cycle_most, w_ph),
        scratch=(pltpu.VMEM((ch_dev * tile_rows, width), BF16), *tables(1)),
        flops=2 * ch_dev * tile_rows * tile_rows * width,
        moved=6 * 2**20,
    )
    returned = exchange(back)
    amp3 = after(amp3, back)
    amp4 = both(amp3[0][: count // 2], amp3[1][count // 2 :])
    ladder_most = most((own_rows, *amp1, *amp2, *amp3), v_pp)
    return call(
        functools.partial(final_kernel, blocks),
        jax.ShapeDtypeStruct((ch_dev, tile_rows, width), BF16),
        (
            coef,
            *amp4,
            ladder_most,
            v_pp,
            returned,
            v_pphh,
            e_part[:, :, None],
            e_hole[:, None, :],
        ),
        (target, pp_size),
        flops=2 * ch_dev * tile_rows * tile_rows * width,
        moved=6 * 2**20,
    )


def solution(mesh):
    placed = (
        P("chan", "tile", None),
        P("chan", "tile", None),
        P("chan", "tile", None),
        P("chan", "tile", None),
        P("chan", "tile"),
        P("chan", "tile"),
        P("chan"),
        P("chan", "tile"),
        P("chan", None),
    )
    return jax.shard_map(
        body, mesh=mesh, in_specs=placed, out_specs=P("chan", "tile", None), check_vma=False
    )
```

```python
import functools

import jax
import jax.numpy as jnp
from jax import lax
from jax.experimental import pallas as pl
from jax.experimental.pallas import tpu as pltpu
from jax.sharding import PartitionSpec as P

META = 128
VMEM_LIMIT = 56 * 1024 * 1024

F32, BF16, I32 = jnp.float32, jnp.bfloat16, jnp.int32


def call(kernel, outs, operands, scalars=(), scratch=(), flops=0, moved=0):
    smem, vmem = pl.BlockSpec(memory_space=pltpu.SMEM), pl.BlockSpec(memory_space=pltpu.VMEM)
    return pl.pallas_call(
        kernel,
        out_shape=outs,
        in_specs=[smem] * len(scalars) + [vmem] * len(operands),
        out_specs=jax.tree.map(lambda _: vmem, outs),
        scratch_shapes=list(scratch),
        compiler_params=pltpu.CompilerParams(vmem_limit_bytes=VMEM_LIMIT),
        cost_estimate=pl.CostEstimate(flops=flops, bytes_accessed=moved, transcendentals=0),
    )(*scalars, *operands)


def tables(count):
    return (
        pltpu.VMEM((count, 8, META), I32),
        pltpu.SMEM((count, 8, META), I32),
        pltpu.SemaphoreType.DMA,
    )


def to_scalars(vector, scalar, sem):
    copy = pltpu.make_async_copy(vector, scalar, sem)
    copy.start()
    copy.wait()


def pack_kernel(blocks, target, coef, amp, items, part_a, part_b):
    count, rows, width = amp.shape
    ch_dev, nb_tile = target.shape
    factor = coef[...].astype(F32)
    part_a[...] = amp[: count // 2]
    part_b[...] = amp[count // 2 :]
    for b in range(count):
        ch, j = divmod(b, nb_tile)
        to = lax.div(target[ch, j], ch_dev * blocks)
        slot = lax.rem(target[ch, j], ch_dev * blocks)
        scaled = amp[b].astype(F32) * factor[ch : ch + 1, j : j + 1]
        items[to, :, :width] = scaled.astype(BF16)
        items[to, :, width:] = jnp.full((rows, META), slot.astype(F32)).astype(BF16)


def settle_kernel(blocks, got, part_a, part_b, homes, placed, slot_v, slot, sem):
    count, rows, wide = got.shape
    width = wide - META
    nb_tile = count // 2
    lane = lax.broadcasted_iota(I32, (rows, META), 1)
    notes = jnp.zeros((rows, META), F32)
    for c in range(count):
        notes = jnp.where(lane == c, got[c, :, width:].astype(F32), notes)
    at = notes[:8].astype(I32)
    homes[...] = lax.div(at, blocks) * nb_tile + lax.rem(at, nb_tile)
    slot_v[0] = homes[...]
    to_scalars(slot_v, slot, sem)
    for c in range(count):
        placed[slot[0, 0, c]] = got[c, :, :width]
    part_a[...] = placed[: count // 2]
    part_b[...] = placed[count // 2 :]


def tile_at(step):
    n = lax.axis_size("tile")
    return lax.rem(lax.axis_index("tile") + step + n, n)


STEPS = (0, -1, 1, -2, 2, -3, 3, 4)


def most_kernel(*refs):
    pieces, (matrix, part, placed) = refs[:-3], refs[-3:]
    ch_dev, total, width = placed.shape
    near = len(STEPS) - 1
    per = total // len(STEPS)
    split = len(pieces) == ch_dev * near
    each = per // pieces[0].shape[1]
    for ch in range(ch_dev):
        for i, step in enumerate(STEPS[:-1]):
            at = pl.ds(pl.multiple_of(tile_at(step) * per, per), per)
            ref = pieces[ch * near + i] if split else pieces[i]
            block = ref[...] if split else ref[ch * each : (ch + 1) * each]
            placed[ch, at] = block.reshape(per, width)
        at = pl.ds(pl.multiple_of(tile_at(STEPS[-1]) * per, per), per)
        placed[ch, at] = jnp.zeros((per, width), BF16)
    for ch in range(ch_dev):
        part[ch] = jnp.dot(matrix[ch], placed[ch], preferred_element_type=F32)


def rest_of(ch, halves, matrix):
    per, width = matrix.shape[1], halves[0].shape[2]
    columns = pl.ds(pl.multiple_of(tile_at(STEPS[-1]) * per, per), per)
    last = halves[ch][...].reshape(per, width)
    return jnp.dot(matrix[ch, :, columns], last, preferred_element_type=F32)


def back_kernel(homes, half_a, half_b, part, w_ph, back, result, slot_v, slot, sem):
    count, rows, _ = back.shape
    ch_dev, per, width = part.shape
    slot_v[0] = homes[...]
    to_scalars(slot_v, slot, sem)
    for ch in range(ch_dev):
        total = part[ch] + rest_of(ch, (half_a, half_b), w_ph)
        result[ch * per : (ch + 1) * per] = total.astype(BF16)
    for c in range(count):
        row = pl.ds(pl.multiple_of(slot[0, 0, c] * rows, rows), rows)
        back[c] = result[row, :]


def final_kernel(
    blocks, target, live, coef, half_a, half_b, part, v_pp, back, v_pphh, e_part, e_hole, out
):
    ch_dev, per, width = out.shape
    count, rows, _ = back.shape
    nb_tile = count // ch_dev
    first = lax.axis_index("tile") * per
    factor = coef[...].astype(F32)
    for ch in range(ch_dev):
        more = rest_of(ch, (half_a, half_b), v_pp)
        for b in range(nb_tile):
            at = slice(b * rows, (b + 1) * rows)
            own = lax.div(target[ch, b], ch_dev * blocks)
            come = back[own].astype(F32) * factor[ch : ch + 1, b : b + 1]
            sums = v_pphh[ch, at].astype(F32) + (part[ch, at] + more[at]) + come
            denom = e_part[ch, at] + e_hole[ch]
            row = lax.broadcasted_iota(I32, (rows, width), 0) + (first + b * rows)
            out[ch, at] = jnp.where(row < live[ch], sums / denom, 0.0).astype(BF16)


def after(x, *others):
    return lax.optimization_barrier((x, *others))[0]


def body(amp, v_pphh, v_pp, w_ph, coef, target, pp_size, e_part, e_hole):
    ch_dev, tile_rows, width = amp.shape
    nb_tile = target.shape[1]
    rows = tile_rows // nb_tile
    n_tile = lax.axis_size("tile")
    blocks = nb_tile * n_tile
    count = ch_dev * nb_tile
    total = tile_rows * n_tile
    right = [(i, (i + 1) % n_tile) for i in range(n_tile)]
    left = [((i + 1) % n_tile, i) for i in range(n_tile)]
    to_right = functools.partial(lax.ppermute, axis_name="tile", perm=right)
    to_left = functools.partial(lax.ppermute, axis_name="tile", perm=left)

    def both(a, b):
        return to_right(a), to_left(b)

    exchange = functools.partial(
        lax.all_to_all, axis_name="chan", split_axis=0, concat_axis=0, tiled=True
    )

    own_rows = amp.reshape(count, rows, width)
    block_type = jax.ShapeDtypeStruct((count, rows, width), BF16)
    part_type = jax.ShapeDtypeStruct((ch_dev, tile_rows, width), F32)
    half = count // ch_dev
    half_type = jax.ShapeDtypeStruct((half, rows, width), BF16)
    items, amp_a, amp_b = call(
        functools.partial(pack_kernel, blocks),
        (jax.ShapeDtypeStruct((count, rows, width + META), BF16), half_type, half_type),
        (coef, own_rows),
        (target,),
        moved=6 * 2**20,
    )
    a1, b1 = both(amp_a, amp_a), both(amp_b, amp_b)
    amp1 = tuple(jnp.concatenate(x, axis=0) for x in zip(a1, b1))
    far_a, far_b, homes = call(
        functools.partial(settle_kernel, blocks),
        (half_type, half_type, jax.ShapeDtypeStruct((8, META), I32)),
        (after(exchange(items), a1),),
        scratch=(pltpu.VMEM((count, rows, width), BF16), *tables(1)),
        flops=10**14,
        moved=4 * 2**20,
    )
    fa1, fb1 = both(*after((far_a, far_a), b1)), both(far_b, far_b)
    amp2 = both(*after(amp1))
    fa2, fb2 = both(*fa1), both(*fb1)
    fa3, fb3 = both(*fa2), both(*fb2)
    far4 = to_right(fa3[0]), to_left(fb3[1])

    def most(pieces, matrix):
        return call(
            most_kernel,
            part_type,
            (*pieces, matrix),
            scratch=(pltpu.VMEM((ch_dev, total, width), BF16),),
            flops=2 * ch_dev * tile_rows * total * width,
            moved=12 * 2**20,
        )

    e_col, e_row = e_part[:, :, None], e_hole[:, None, :]
    cycle_most = most((far_a, *fa1, *fa2, *fa3, far_b, *fb1, *fb2, *fb3), after(w_ph, e_col, e_row))
    amp3 = both(*after(amp2, cycle_most, far4))
    back = call(
        back_kernel,
        block_type,
        (homes, *far4, cycle_most, w_ph),
        scratch=(pltpu.VMEM((ch_dev * tile_rows, width), BF16), *tables(1)),
        flops=2 * ch_dev * tile_rows * tile_rows * width,
        moved=6 * 2**20,
    )
    returned = exchange(back)
    amp3 = after(amp3, back)
    amp4 = both(amp3[0][: count // 2], amp3[1][count // 2 :])
    ladder_most = most((own_rows, *amp1, *amp2, *amp3), v_pp)
    return call(
        functools.partial(final_kernel, blocks),
        jax.ShapeDtypeStruct((ch_dev, tile_rows, width), BF16),
        (
            coef,
            *amp4,
            ladder_most,
            v_pp,
            returned,
            v_pphh,
            e_col,
            e_row,
        ),
        (target, pp_size),
        flops=2 * ch_dev * tile_rows * tile_rows * width,
        moved=6 * 2**20,
    )


def solution(mesh):
    placed = (
        P("chan", "tile", None),
        P("chan", "tile", None),
        P("chan", "tile", None),
        P("chan", "tile", None),
        P("chan", "tile"),
        P("chan", "tile"),
        P("chan"),
        P("chan", "tile"),
        P("chan", None),
    )
    return jax.shard_map(
        body, mesh=mesh, in_specs=placed, out_specs=P("chan", "tile", None), check_vma=False
    )
```
